512 devices in a mesh: dp: 16 (over z_hi, x), lat: 32 (over y, z_lo, core).
Axes of the slice: x: 4, y: 4, z: 16 (z_hi: 4, z_lo: 4; z = z_hi * 4 + z_lo), core: 2. Of those that a mesh axis runs over, the one named last changes fastest.
Arguments:
- states: bfloat16 [16, 128, 128, 128], P('dp', 'lat'), may hold values from -6 to 6
- basis_table: bfloat16 [128, 25, 9, 5], replicated, may hold values from -1.1953125 to 1.1953125
- offsets: int32 [128], replicated, may hold values from -12 to -8, as said below
- widths: int32 [128], replicated, may hold values from 21 to 25, as said below
- mixing: bfloat16 [9, 128, 128], replicated, may hold values from -0.1875 to 0.1875
- cotangent: bfloat16 [16, 128, 128, 128], P('dp', 'lat'), may hold values from -6 to 6
Outputs:
- output: bfloat16 [16, 128, 128, 128], P('dp', 'lat')
- grad_states: bfloat16 [16, 128, 128, 128], P('dp', 'lat')
- grad_mixing: float32 [9, 128, 128], replicated
The draws below stay inside these ranges and needn't reach their ends.
Inputs may be any that keep to these rules, and one draw needn't show every extreme that they name: The support of every output latitude o contains o itself and lies within latitudes o - 12 to o + 12, so offsets[o] is at most 13 - widths[o]. widths is 25 at the two pole latitudes 0 and 127.
All inputs are finite; a program needn't handle non-finite values.
Results may differ from the reference program's by a relative error of at most 0.0049.
Values may be sent and summed in bfloat16 or wider, within the bound.
No kernel may reach another device: no remote copies, remote signals or barrier semaphores. Data moves between devices by JAX's collectives and lax.ppermute only.
A program may use at most 64 MiB of HBM per device.

```python
import math
import jax
import jax.numpy as jnp
from jax import lax

BAND_ROWS = 4
LONGITUDES = 128
CHANNELS = 128
BASIS = 9
TAPS = 5
HALO = 12
SUPPORT = 25
LATITUDES = 128
SAMPLES = 16
N_LAT = 32


def support_table(key):
    support = 2 * HALO + 1
    latitude_ids = jnp.arange(LATITUDES, dtype=jnp.int32)
    distance = jnp.minimum(latitude_ids, LATITUDES - 1 - latitude_ids)
    jitter = jax.random.randint(jax.random.fold_in(key, 11), (LATITUDES,), 0, 5, dtype=jnp.int32)
    widths = support - jitter
    widths = jnp.where(distance == 0, support, widths)
    widths = jnp.where(latitude_ids == LATITUDES // 2, support - 4, widths)
    nudge = jax.random.randint(jax.random.fold_in(key, 23), (LATITUDES,), -1, 2, dtype=jnp.int32)
    centred = -(widths // 2) + nudge
    offsets = jnp.clip(centred, -HALO, HALO - widths + 1)
    offsets = jnp.minimum(offsets, 0)
    highest = min(0, 4 - HALO)
    offsets = jnp.where(latitude_ids == LATITUDES // 2, highest, offsets)
    return (offsets.astype(jnp.int32), widths.astype(jnp.int32))


def draw_offsets(key, part):
    return support_table(key)[0]


def draw_widths(key, part):
    return support_table(key)[1]


def level_of(rng, shape, split, smallest, top_value):
    factor_of = 1.0
    for dim, parts in split:
        draws = jax.random.uniform(jax.random.fold_in(jax.random.fold_in(rng, 6), dim), (parts,), jnp.float32, smallest / len(split), top_value / len(split))
        factor_of = factor_of * jnp.repeat(jnp.exp(draws), shape[dim] // parts).reshape((-1,) + (1,) * (len(shape) - 1 - dim))
    return factor_of


def noise(stream_key, extent, width, limit, split=(), held_as=jnp.bfloat16):
    array = width * jax.random.normal(stream_key, extent, jnp.float32)
    if split:
        array = array * level_of(stream_key, extent, split, -0.22, 0.18)
    return jnp.clip(array, -limit, limit).astype(held_as)


def setup_inputs(seed: int = 0) -> dict:
    keys = jax.random.split(jax.random.key(seed), 7)
    states = noise(keys[0], (SAMPLES, LATITUDES, LONGITUDES, CHANNELS), 1.0, 6.0, ((0, 16), (1, 32)))
    basis_table = noise(keys[1], (LATITUDES, SUPPORT, BASIS, TAPS), 0.2, 1.1953125)
    offsets = draw_offsets(jax.random.fold_in(keys[6], 71), 0)
    widths = draw_widths(jax.random.fold_in(keys[6], 71), 0)
    mixing = noise(keys[4], (BASIS, CHANNELS, CHANNELS), (BASIS * CHANNELS) ** -0.5, 0.1875)
    cotangent = noise(keys[5], (SAMPLES, LATITUDES, LONGITUDES, CHANNELS), 1.0, 6.0, ((0, 16), (1, 32)))
    return dict(states=states, basis_table=basis_table, offsets=offsets, widths=widths, mixing=mixing, cotangent=cotangent)


def band_matrix(table_rows, offsets, widths, ext_rows, offset_base):
    out_rows = offsets.shape[0]
    support = table_rows.shape[1]
    slot_ids = jnp.arange(support, dtype=jnp.int32)
    target = jnp.arange(out_rows, dtype=jnp.int32)[:, None] + offset_base + offsets[:, None] + slot_ids[None, :]
    column = jnp.arange(ext_rows, dtype=jnp.int32)
    matches = (target[:, :, None] == column[None, None, :]) & (slot_ids[None, :, None] < widths[:, None, None])
    return jnp.einsum('qskt,qse->ktqe', table_rows.astype(jnp.float32), matches.astype(jnp.float32)).astype(jnp.bfloat16)

def reference(states, basis_table, offsets, widths, mixing, cotangent):
    half_taps = TAPS // 2
    ext_rows = BAND_ROWS + 2 * HALO
    weights = mixing.astype(jnp.float32)

    def one_sample(carry, pair):
        sample_state, sample_cot = pair
        padded = jnp.pad(sample_state, ((HALO, HALO), (0, 0), (0, 0)))

        def one_band(inner, band_index):
            grad_pad, grad_sum = inner
            first_row = (band_index * BAND_ROWS).astype(jnp.int32)
            window = lax.dynamic_slice_in_dim(padded, first_row, ext_rows, 0)
            matrix = band_matrix(lax.dynamic_slice_in_dim(basis_table, first_row, BAND_ROWS, 0), lax.dynamic_slice_in_dim(offsets, first_row, BAND_ROWS, 0), lax.dynamic_slice_in_dim(widths, first_row, BAND_ROWS, 0), ext_rows, HALO)
            rolled = jnp.stack([jnp.roll(window, half_taps - tap_index, axis=1) for tap_index in range(TAPS)])
            filtered = jnp.einsum('ktqe,telc->kqlc', matrix.astype(jnp.float32), rolled.astype(jnp.float32)).astype(jnp.bfloat16)
            band_out = jnp.einsum('kqlc,kcd->qld', filtered.astype(jnp.float32), weights).astype(jnp.bfloat16)
            band_cot = lax.dynamic_slice_in_dim(sample_cot, first_row, BAND_ROWS, 0).astype(jnp.float32)
            grad_filtered = jnp.einsum('qld,kcd->kqlc', band_cot, weights).astype(jnp.bfloat16)
            grad_sum = grad_sum + jnp.einsum('kqlc,qld->kcd', filtered.astype(jnp.float32), band_cot)
            partial_value = jnp.zeros((ext_rows, LONGITUDES, CHANNELS), jnp.float32)
            for tap_index in range(TAPS):
                term = jnp.einsum('kqe,kqlc->elc', matrix[:, tap_index].astype(jnp.float32), grad_filtered.astype(jnp.float32))
                partial_value = partial_value + jnp.roll(term, tap_index - half_taps, axis=1)
            current = lax.dynamic_slice_in_dim(grad_pad, first_row, ext_rows, 0)
            grad_pad = lax.dynamic_update_slice_in_dim(grad_pad, current + partial_value, first_row, 0)
            return ((grad_pad, grad_sum), band_out)
        grad_start = jnp.zeros((LATITUDES + 2 * HALO, LONGITUDES, CHANNELS), jnp.float32)
        (grad_pad, grad_sum), bands = lax.scan(one_band, (grad_start, carry), jnp.arange(N_LAT, dtype=jnp.int32))
        sample_out = bands.reshape(LATITUDES, LONGITUDES, CHANNELS)
        sample_grad = grad_pad[HALO:HALO + LATITUDES].astype(jnp.bfloat16)
        return (grad_sum, (sample_out, sample_grad))
    total_start = jnp.zeros((BASIS, CHANNELS, CHANNELS), jnp.float32)
    total, (output, grad_states) = lax.scan(one_sample, total_start, (states, cotangent))
    grad_mixing = total * (1.0 / math.sqrt(SAMPLES * LATITUDES * LONGITUDES))
    return (output, grad_states, grad_mixing)
```

```python
import math

import jax
import jax.numpy as jnp
from jax import lax
from jax.sharding import Mesh, PartitionSpec as P

TAPS = 5
HALO = 12
DP = ("z_hi", "x")
LAT = ("y", "z_lo", "core")
PLANE = ("x", "y", "core")
RING = ("z_hi", "z_lo")


def summed_everywhere(local):
    plane = lax.axis_size(PLANE)
    ring = lax.axis_size(RING)
    parts = local.astype(jnp.bfloat16).reshape(plane, -1, local.shape[-1])
    part = lax.all_to_all(parts, PLANE, 0, 0).astype(jnp.float32).sum(0).astype(jnp.bfloat16)
    terms = lax.all_to_all(jnp.broadcast_to(part[None], (ring,) + part.shape), RING, 0, 0)
    part = terms.astype(jnp.float32).sum(0).astype(jnp.bfloat16)
    whole = lax.all_to_all(jnp.broadcast_to(part[None], (plane,) + part.shape), PLANE, 0, 0)
    return whole.astype(jnp.float32).reshape(local.shape)


def shifted(x, axis, by):
    count = lax.axis_size(axis)
    pairs = [(i, i + by) for i in range(count) if 0 <= i + by < count]
    return lax.ppermute(x, axis, pairs)


def band_matrix(table_rows, offsets, widths, ext_rows, offset_base):
    out_rows = offsets.shape[0]
    support = table_rows.shape[1]
    slot_ids = jnp.arange(support, dtype=jnp.int32)
    target = (
        jnp.arange(out_rows, dtype=jnp.int32)[:, None]
        + offset_base
        + offsets[:, None]
        + slot_ids[None, :]
    )
    column = jnp.arange(ext_rows, dtype=jnp.int32)
    matches = (target[:, :, None] == column[None, None, :]) & (
        slot_ids[None, :, None] < widths[:, None, None]
    )
    return jnp.einsum(
        "qskt,qse->ktqe",
        table_rows,
        matches.astype(jnp.bfloat16),
        preferred_element_type=jnp.float32,
    ).astype(jnp.bfloat16)


def halo_rows(stacked, axis_rows):
    band_rows = stacked.shape[axis_rows]
    hop_count = -(-HALO // band_rows)
    above = []
    for distance in range(hop_count, 0, -1):
        row_count = min(band_rows, HALO - (distance - 1) * band_rows)
        piece = stacked
        above.append(shifted(piece, LAT, distance))
    below = []
    for distance in range(1, hop_count + 1):
        row_count = min(band_rows, HALO - (distance - 1) * band_rows)
        piece = stacked
        below.append(shifted(piece, LAT, -distance))
    return jnp.concatenate(above + [stacked] + below, axis=axis_rows)


def adjoint_rows(matrix, grad_filtered, half_taps):
    total = None
    for tap_index in range(TAPS):
        term = jnp.einsum(
            "kqe,bkqlc->belc",
            matrix[:, tap_index],
            grad_filtered,
            preferred_element_type=jnp.float32,
        )
        term = jnp.roll(term, tap_index - half_taps, axis=2)
        total = term if total is None else total + term
    return total


def shards(states, basis_table, offsets, widths, mixing, cotangent):
    band_rows = states.shape[1]
    half_taps = TAPS // 2
    ext_rows = band_rows + 2 * HALO
    first_row = lax.axis_index(LAT) * band_rows
    table_rows = lax.dynamic_slice_in_dim(basis_table, first_row, band_rows, 0)
    own_offsets = lax.dynamic_slice_in_dim(offsets, first_row, band_rows, 0)
    own_widths = lax.dynamic_slice_in_dim(widths, first_row, band_rows, 0)
    both_ext = halo_rows(jnp.stack((states, cotangent)), 2)
    states_ext = both_ext[0]
    cot_ext = both_ext[1]
    forward_matrix = band_matrix(table_rows, own_offsets, own_widths, ext_rows, HALO)
    rolled = jnp.stack(
        [jnp.roll(states_ext, half_taps - tap_index, axis=2) for tap_index in range(TAPS)], axis=1
    )
    filtered = jnp.einsum(
        "ktqe,btelc->bkqlc", forward_matrix, rolled, preferred_element_type=jnp.float32
    ).astype(jnp.bfloat16)
    output = jnp.einsum(
        "bkqlc,kcd->bqld", filtered, mixing, preferred_element_type=jnp.float32
    ).astype(jnp.bfloat16)
    grad_ext = jnp.einsum(
        "bqld,kcd->bkqlc", cot_ext, mixing, preferred_element_type=jnp.float32
    ).astype(jnp.bfloat16)
    table_pad = jnp.pad(basis_table, ((HALO, HALO), (0, 0), (0, 0), (0, 0)))
    offset_pad = jnp.pad(offsets, ((HALO, HALO),))
    width_pad = jnp.pad(widths, ((HALO, HALO),))
    adjoint_matrix = band_matrix(
        lax.dynamic_slice_in_dim(table_pad, first_row, ext_rows, 0),
        lax.dynamic_slice_in_dim(offset_pad, first_row, ext_rows, 0),
        lax.dynamic_slice_in_dim(width_pad, first_row, ext_rows, 0),
        band_rows,
        -HALO,
    )
    grad_states = adjoint_rows(adjoint_matrix, grad_ext, half_taps).astype(jnp.bfloat16)
    grad_local = jnp.einsum(
        "bkqlc,bqld->kcd", filtered, cotangent, preferred_element_type=jnp.float32
    )
    cell_count = (
        states.shape[0] * lax.axis_size(DP) * band_rows * lax.axis_size(LAT) * states.shape[2]
    )
    grad_scale = 1.0 / math.sqrt(cell_count)
    grad_mixing = summed_everywhere(grad_local) * grad_scale
    return (output, grad_states, grad_mixing)


def solution(mesh):
    fine = Mesh(mesh.devices.reshape(4, 4, 4, 4, 2), DP + LAT)
    banded = P(DP, LAT, None, None)
    in_specs = (banded, P(), P(), P(), P(), banded)
    out_specs = (banded, banded, P())
    return jax.shard_map(shards, mesh=fine, in_specs=in_specs, out_specs=out_specs, check_vma=False)
```

```python
import math

import jax
import jax.numpy as jnp
from jax import lax
from jax.experimental import pallas as pl
from jax.experimental.pallas import tpu as pltpu
from jax.sharding import Mesh, PartitionSpec as P

TAPS = 5
GROUP = 4
WINDOW = GROUP + TAPS - 1
PART = 48
DP = ("z_hi", "x")
LAT = ("y", "z_lo", "core")
PLANE = ("x", "y", "core")
RING = ("z_hi", "z_lo")
SLOTS = ((-3, -2, -1, 0, 1, 2, 3), (3, -2, -3, 0, -1, 2, 1))
VMEM = pl.BlockSpec(memory_space=pltpu.VMEM)
SMEM = pl.BlockSpec(memory_space=pltpu.SMEM)
hold = lax.optimization_barrier


def call(kernel, outs, scratch, flops, *args, scalars=0):
    moved = sum(x.size * x.dtype.itemsize for x in tuple(args) + tuple(outs))
    return pl.pallas_call(
        kernel,
        out_shape=outs,
        in_specs=[SMEM] * scalars + [VMEM] * (len(args) - scalars),
        out_specs=[VMEM] * len(outs),
        scratch_shapes=scratch,
        compiler_params=pltpu.CompilerParams(vmem_limit_bytes=40 * 1024 * 1024),
        cost_estimate=pl.CostEstimate(flops=flops, bytes_accessed=moved, transcendentals=0),
    )(*args)


def by_longitude(x_ref, wide, rows, cells):
    for r in range(rows):
        wide[pl.ds(2 * rows + r, cells, stride=rows), :] = x_ref[r].astype(jnp.float32)
    edge = 2 * rows
    wide[0:edge, :] = wide[cells * rows : cells * rows + edge, :]
    wide[cells * rows + edge : cells * rows + 2 * edge, :] = wide[edge : 2 * edge, :]


def prepare_kernel(states_ref, cot_ref, both_out, own_out, wide):
    rows, cells, _ = states_ref.shape
    tall = wide.shape[0]
    by_longitude(states_ref, wide, rows, cells)
    both_out[:tall, :] = wide[...].astype(both_out.dtype)
    by_longitude(cot_ref, wide, rows, cells)
    both_out[tall:, :] = wide[...].astype(both_out.dtype)
    own_out[...] = wide[2 * rows : 2 * rows + cells * rows, :].astype(own_out.dtype)


def spread(rows, column, taken, out_ref):
    taps, pairs, latitudes = taken.shape
    height, width = out_ref.shape
    out_row = lax.broadcasted_iota(jnp.int32, (height, pairs), 0)
    pair = lax.broadcasted_iota(jnp.int32, (height, pairs), 1)
    block = GROUP * rows
    one = lambda x: x.astype(jnp.float32).astype(jnp.bfloat16)
    pick = one(out_row // block * rows + out_row % rows == pair)
    copy = one(lax.broadcasted_iota(jnp.int32, (latitudes, width), 0) == column)
    lane = lax.broadcasted_iota(jnp.int32, (height, width), 1)
    line = lax.broadcasted_iota(jnp.int32, (height, width), 0)
    step = lane // rows % WINDOW - line // rows % GROUP
    total = jnp.zeros((height, width), jnp.float32)
    for t in range(taps):
        tall = jnp.dot(pick, one(taken[t]), preferred_element_type=jnp.float32).astype(jnp.bfloat16)
        full = jnp.dot(tall, copy, preferred_element_type=jnp.float32)
        total = jnp.where(step == t, full, total)
    out_ref[...] = total.astype(out_ref.dtype)


def forward_table_kernel(rows, first_ref, offset_ref, width_ref, column_ref, table_ref, out_ref, padded, taken):
    basis, taps, support, latitudes = table_ref.shape
    depth = padded.shape[0] // taps
    slot = lax.broadcasted_iota(jnp.int32, (depth, latitudes), 0)
    latitude = lax.broadcasted_iota(jnp.int32, (depth, latitudes), 1)
    source = lax.broadcasted_iota(jnp.int32, (latitudes, latitudes), 0)
    first = first_ref[0]
    masks, spreads = [], []
    for q in range(rows):
        own = first + q
        masks.append((slot == latitude - own - offset_ref[own]) & (slot < width_ref[own]))
        spreads.append((source == own).astype(jnp.float32).astype(jnp.bfloat16))
    spreads = jnp.concatenate(spreads, axis=1)
    padded[...] = jnp.zeros_like(padded)
    taken[...] = jnp.zeros_like(taken)
    for k in range(basis):
        for t in range(taps):
            padded[t * depth : t * depth + support, :] = table_ref[k, t].astype(jnp.float32)
        every = jnp.dot(padded[...].astype(jnp.bfloat16), spreads, preferred_element_type=jnp.float32)
        for t in range(taps):
            for q in range(rows):
                values = every[t * depth : (t + 1) * depth, q * latitudes : (q + 1) * latitudes]
                row = jnp.sum(jnp.where(masks[q], values, 0.0), axis=0, keepdims=True)
                taken[t, k * rows + q : k * rows + q + 1, :] = row
    spread(rows, column_ref[...], taken, out_ref)


def adjoint_table_kernel(rows, first_ref, offset_ref, width_ref, column_ref, table_ref, out_ref, taken):
    basis, taps, support, latitudes = table_ref.shape
    slot = lax.broadcasted_iota(jnp.int32, (support, latitudes), 0)
    latitude = lax.broadcasted_iota(jnp.int32, (support, latitudes), 1)
    live = slot < width_ref[...]
    start = latitude + offset_ref[...]
    masks = [live & (slot == first_ref[0] + i - start) for i in range(rows)]
    taken[...] = jnp.zeros_like(taken)
    for k in range(basis):
        for t in range(taps):
            values = table_ref[k, t].astype(jnp.float32)
            for i in range(rows):
                row = jnp.sum(jnp.where(masks[i], values, 0.0), axis=0, keepdims=True)
                taken[taps - 1 - t, k * rows + i : k * rows + i + 1, :] = row
    spread(rows, column_ref[...], taken, out_ref)


def filter_bands(pieces, first, matrix, rows, basis, out_ref):
    block = GROUP * rows
    reach = WINDOW * rows
    channels = pieces[0].shape[1]
    groups = out_ref.shape[0] // block
    table = matrix[...]
    for g in range(0, groups, 2):
        halves = [
            jnp.concatenate([p[first + h * block : first + h * block + reach, :] for p in pieces], axis=0)
            for h in (g, g + 1)
        ]
        both = jnp.dot(
            table, jnp.concatenate(halves, axis=1), preferred_element_type=jnp.float32
        ).astype(out_ref.dtype)
        for half in range(2):
            for k in range(basis):
                out_ref[(g + half) * block : (g + half + 1) * block, k * channels : (k + 1) * channels] = both[
                    k * block : (k + 1) * block, half * channels : (half + 1) * channels
                ]


def forward_kernel(rows, *refs):
    pieces = refs[:7]
    matrix, own, filtered, grad = refs[7:]
    channels = own.shape[1]
    basis = filtered.shape[1] // channels
    filter_bands(pieces, 0, matrix, rows, basis, filtered)
    turned = lax.dot_general(
        own[...], filtered[...], (((0,), (0,)), ((), ())), preferred_element_type=jnp.float32
    )
    for k in range(basis):
        grad[k * channels : (k + 1) * channels, :] = turned[:, k * channels : (k + 1) * channels].T.astype(
            grad.dtype
        )
    used = basis * channels
    grad[used:, :] = jnp.zeros((grad.shape[0] - used, channels), grad.dtype)


def by_row(value, wide, out_ref):
    rows, cells, _ = out_ref.shape
    wide[...] = value
    for r in range(rows):
        out_ref[r] = wide[pl.ds(r, cells, stride=rows), :].astype(out_ref.dtype)


def backward_kernel(rows, *refs):
    pieces = refs[:7]
    matrix, filtered, mixing, output, grad_states, turned, wide = refs[7:]
    basis, channels, _ = mixing.shape
    by_row(
        jnp.dot(
            filtered[...],
            mixing[...].reshape(basis * channels, channels),
            preferred_element_type=jnp.float32,
        ),
        wide,
        output,
    )
    filter_bands(pieces, pieces[0].shape[0] // 2, matrix, rows, basis, turned)
    total = None
    for k in range(basis):
        term = lax.dot_general(
            turned[:, k * channels : (k + 1) * channels],
            mixing[k],
            (((1,), (1,)), ((), ())),
            preferred_element_type=jnp.float32,
        )
        total = term if total is None else total + term
    by_row(total, wide, grad_states)


def chips_apart(x):
    return lax.ppermute(x, LAT, steps(2)), lax.ppermute(x, LAT, steps(-2))


def far_and_near(x):
    far = [p for p in steps(3) if p[0] % 2 == 1] + [p for p in steps(-3) if p[0] % 2 == 0]
    return lax.ppermute(x, LAT, far), from_mate(x)


def from_mate(x):
    return lax.ppermute(x, LAT, [(i, i ^ 1) for i in range(lax.axis_size(LAT))])


def steps(by):
    count = lax.axis_size(LAT)
    return [(i, i + by) for i in range(count) if 0 <= i + by < count]


def scattered(parts):
    return lax.all_to_all(parts, PLANE, 0, 0).astype(jnp.float32).sum(0).astype(jnp.bfloat16)


def gathered(part, axes):
    return lax.all_to_all(jnp.broadcast_to(part[None], (lax.axis_size(axes),) + part.shape), axes, 0, 0)


def shards(states, basis_table, offsets, widths, mixing, cotangent):
    _, rows, cells, channels = states.shape
    basis = mixing.shape[0]
    first_row = lax.axis_index(LAT) * rows
    bf16 = jnp.bfloat16
    tall = jax.ShapeDtypeStruct((2 * (cells + TAPS - 1) * rows, channels), bf16)
    flat = jax.ShapeDtypeStruct((cells * rows, channels), bf16)
    both, cot_own = call(
        prepare_kernel,
        [tall, flat],
        [pltpu.VMEM((tall.shape[0] // 2, channels), jnp.float32)],
        0,
        states[0],
        cotangent[0],
    )
    before, after = chips_apart(both)
    far, mate = far_and_near(both)

    support, latitudes = basis_table.shape[1], basis_table.shape[0]
    table = basis_table.transpose(2, 3, 1, 0)
    band = jnp.where(lax.axis_index("core") == 0, jnp.array(SLOTS[0]), jnp.array(SLOTS[1]))
    column = first_row + band[:, None, None] * rows + jnp.arange(rows)[None, None, :]
    width = len(SLOTS[0]) * WINDOW * rows
    column = jnp.broadcast_to(column, (len(SLOTS[0]), WINDOW, rows)).reshape(1, width).astype(jnp.int32)
    matrix = jax.ShapeDtypeStruct((basis * GROUP * rows, width), bf16)
    first = first_row.astype(jnp.int32)[None]
    depth = -(-support // 8) * 8
    pairs = -(-basis * rows // 8) * 8
    taken = pltpu.VMEM((TAPS, pairs, latitudes), jnp.float32)
    (forward_wide,) = call(
        lambda *refs: forward_table_kernel(rows, *refs),
        [matrix],
        [pltpu.VMEM((TAPS * depth, latitudes), jnp.float32), taken],
        400_000_000,
        first,
        offsets,
        widths,
        column,
        table,
        scalars=3,
    )
    (adjoint_wide,) = call(
        lambda *refs: adjoint_table_kernel(rows, *refs),
        [matrix],
        [taken],
        400_000_000,
        first,
        offsets[None],
        widths[None],
        column,
        table,
        scalars=1,
    )

    before, after, forward_wide = hold((before, after, forward_wide))
    bands = (far, before, from_mate(before), both, mate, after, from_mate(after))
    plane = lax.axis_size(PLANE)
    filtered, grad = call(
        lambda *refs: forward_kernel(rows, *refs),
        [
            jax.ShapeDtypeStruct((cells * rows, basis * channels), bf16),
            jax.ShapeDtypeStruct((plane * PART, channels), bf16),
        ],
        [],
        2_000_000_000,
        *bands,
        forward_wide,
        cot_own,
    )
    part = scattered(grad.reshape(plane, PART, channels))
    part = gathered(part, RING).astype(jnp.float32).sum(0).astype(bf16)
    total = gathered(part, PLANE)
    output, grad_states = call(
        lambda *refs: backward_kernel(rows, *refs),
        [jax.ShapeDtypeStruct(states.shape[1:], bf16)] * 2,
        [
            pltpu.VMEM((cells * rows, basis * channels), bf16),
            pltpu.VMEM((cells * rows, channels), jnp.float32),
        ],
        3_000_000_000,
        *bands,
        adjoint_wide,
        filtered,
        mixing,
    )
    cell_count = lax.axis_size(DP) * rows * lax.axis_size(LAT) * cells
    grad_scale = 1.0 / math.sqrt(cell_count)
    whole = total.reshape(-1, channels)[: basis * channels].reshape(basis, channels, channels)
    return (output[None], grad_states[None], whole.astype(jnp.float32) * grad_scale)


def solution(mesh):
    fine = Mesh(mesh.devices.reshape(4, 4, 4, 4, 2), DP + LAT)
    banded = P(DP, LAT, None, None)
    in_specs = (banded, P(), P(), P(), P(), banded)
    out_specs = (banded, banded, P())
    return jax.shard_map(shards, mesh=fine, in_specs=in_specs, out_specs=out_specs, check_vma=False)
```

```python
import math

import jax
import jax.numpy as jnp
from jax import lax
from jax.experimental import pallas as pl
from jax.experimental.pallas import tpu as pltpu
from jax.sharding import Mesh, PartitionSpec as P

TAPS = 5
GROUP = 4
WINDOW = GROUP + TAPS - 1
PART = 40
DP = ("z_hi", "x")
LAT = ("y", "z_lo", "core")
PLANE = ("x", "y", "core")
RING = ("z_hi", "z_lo")
SLOTS = ((-3, -2, -1, 0, 1, 2, 3), (3, -2, -3, 0, -1, 2, 1))
VMEM = pl.BlockSpec(memory_space=pltpu.VMEM)
SMEM = pl.BlockSpec(memory_space=pltpu.SMEM)
hold = lax.optimization_barrier


def call(kernel, outs, scratch, flops, *args, scalars=0):
    moved = sum(x.size * x.dtype.itemsize for x in tuple(args) + tuple(outs))
    return pl.pallas_call(
        kernel,
        out_shape=outs,
        in_specs=[SMEM] * scalars + [VMEM] * (len(args) - scalars),
        out_specs=[VMEM] * len(outs),
        scratch_shapes=scratch,
        compiler_params=pltpu.CompilerParams(vmem_limit_bytes=40 * 1024 * 1024),
        cost_estimate=pl.CostEstimate(flops=flops, bytes_accessed=moved, transcendentals=0),
    )(*args)


def by_longitude(x_ref, wide, rows, cells):
    for r in range(rows):
        wide[pl.ds(2 * rows + r, cells, stride=rows), :] = x_ref[r].astype(jnp.float32)
    edge = 2 * rows
    wide[0:edge, :] = wide[cells * rows : cells * rows + edge, :]
    wide[cells * rows + edge : cells * rows + 2 * edge, :] = wide[edge : 2 * edge, :]


def prepare_kernel(states_ref, cot_ref, states_out, cot_out, own_out, wide):
    rows, cells, _ = states_ref.shape
    by_longitude(states_ref, wide, rows, cells)
    states_out[...] = wide[...].astype(states_out.dtype)
    by_longitude(cot_ref, wide, rows, cells)
    cot_out[...] = wide[...].astype(cot_out.dtype)
    own_out[...] = wide[2 * rows : 2 * rows + cells * rows, :].astype(own_out.dtype)


def spread(rows, column, taken, out_ref):
    taps, pairs, latitudes = taken.shape
    height, width = out_ref.shape
    out_row = lax.broadcasted_iota(jnp.int32, (height, pairs), 0)
    pair = lax.broadcasted_iota(jnp.int32, (height, pairs), 1)
    block = GROUP * rows
    one = lambda x: x.astype(jnp.float32).astype(jnp.bfloat16)
    pick = one(out_row // block * rows + out_row % rows == pair)
    copy = one(lax.broadcasted_iota(jnp.int32, (latitudes, width), 0) == column)
    lane = lax.broadcasted_iota(jnp.int32, (height, width), 1)
    line = lax.broadcasted_iota(jnp.int32, (height, width), 0)
    step = lane // rows % WINDOW - line // rows % GROUP
    total = jnp.zeros((height, width), jnp.float32)
    for t in range(taps):
        tall = jnp.dot(pick, one(taken[t]), preferred_element_type=jnp.float32).astype(jnp.bfloat16)
        full = jnp.dot(tall, copy, preferred_element_type=jnp.float32)
        total = jnp.where(step == t, full, total)
    out_ref[...] = total.astype(out_ref.dtype)


def forward_table_kernel(rows, first_ref, offset_ref, width_ref, column_ref, table_ref, out_ref, padded, taken):
    basis, taps, support, latitudes = table_ref.shape
    depth = padded.shape[0] // taps
    slot = lax.broadcasted_iota(jnp.int32, (depth, latitudes), 0)
    latitude = lax.broadcasted_iota(jnp.int32, (depth, latitudes), 1)
    source = lax.broadcasted_iota(jnp.int32, (latitudes, latitudes), 0)
    first = first_ref[0]
    masks, spreads = [], []
    for q in range(rows):
        own = first + q
        masks.append((slot == latitude - own - offset_ref[own]) & (slot < width_ref[own]))
        spreads.append((source == own).astype(jnp.float32).astype(jnp.bfloat16))
    spreads = jnp.concatenate(spreads, axis=1)
    padded[...] = jnp.zeros_like(padded)
    taken[...] = jnp.zeros_like(taken)
    for k in range(basis):
        for t in range(taps):
            padded[t * depth : t * depth + support, :] = table_ref[k, t].astype(jnp.float32)
        every = jnp.dot(padded[...].astype(jnp.bfloat16), spreads, preferred_element_type=jnp.float32)
        for t in range(taps):
            for q in range(rows):
                values = every[t * depth : (t + 1) * depth, q * latitudes : (q + 1) * latitudes]
                row = jnp.sum(jnp.where(masks[q], values, 0.0), axis=0, keepdims=True)
                taken[t, k * rows + q : k * rows + q + 1, :] = row
    spread(rows, column_ref[...], taken, out_ref)


def adjoint_table_kernel(rows, first_ref, offset_ref, width_ref, column_ref, table_ref, out_ref, taken):
    basis, taps, support, latitudes = table_ref.shape
    slot = lax.broadcasted_iota(jnp.int32, (support, latitudes), 0)
    latitude = lax.broadcasted_iota(jnp.int32, (support, latitudes), 1)
    live = slot < width_ref[...]
    start = latitude + offset_ref[...]
    masks = [live & (slot == first_ref[0] + i - start) for i in range(rows)]
    taken[...] = jnp.zeros_like(taken)
    for k in range(basis):
        for t in range(taps):
            values = table_ref[k, t].astype(jnp.float32)
            for i in range(rows):
                row = jnp.sum(jnp.where(masks[i], values, 0.0), axis=0, keepdims=True)
                taken[taps - 1 - t, k * rows + i : k * rows + i + 1, :] = row
    spread(rows, column_ref[...], taken, out_ref)


def filter_bands(pieces, first, matrix, rows, basis, out_ref):
    block = GROUP * rows
    reach = WINDOW * rows
    channels = pieces[0].shape[1]
    groups = out_ref.shape[0] // block
    table = matrix[...]
    for g in range(0, groups, 2):
        halves = [
            jnp.concatenate([p[first + h * block : first + h * block + reach, :] for p in pieces], axis=0)
            for h in (g, g + 1)
        ]
        both = jnp.dot(
            table, jnp.concatenate(halves, axis=1), preferred_element_type=jnp.float32
        ).astype(out_ref.dtype)
        for half in range(2):
            for k in range(basis):
                out_ref[(g + half) * block : (g + half + 1) * block, k * channels : (k + 1) * channels] = both[
                    k * block : (k + 1) * block, half * channels : (half + 1) * channels
                ]


def forward_kernel(rows, *refs):
    pieces = refs[:7]
    matrix, own, grad, filtered = refs[7:]
    channels = own.shape[1]
    basis = filtered.shape[1] // channels
    filter_bands(pieces, 0, matrix, rows, basis, filtered)
    turned = lax.dot_general(
        own[...], filtered[...], (((0,), (0,)), ((), ())), preferred_element_type=jnp.float32
    )
    for k in range(basis):
        grad[k * channels : (k + 1) * channels, :] = turned[:, k * channels : (k + 1) * channels].T.astype(
            grad.dtype
        )
    used = basis * channels
    grad[used:, :] = jnp.zeros((grad.shape[0] - used, channels), grad.dtype)


def by_row(value, wide, out_ref):
    rows, cells, _ = out_ref.shape
    wide[...] = value
    for r in range(rows):
        out_ref[r] = wide[pl.ds(r, cells, stride=rows), :].astype(out_ref.dtype)


def backward_kernel(rows, *refs):
    pieces, cot_pieces = refs[:7], refs[7:14]
    forward, adjoint, mixing, output, grad_states, filtered, wide = refs[14:]
    basis, channels, _ = mixing.shape
    filter_bands(pieces, 0, forward, rows, basis, filtered)
    by_row(
        jnp.dot(
            filtered[...],
            mixing[...].reshape(basis * channels, channels),
            preferred_element_type=jnp.float32,
        ),
        wide,
        output,
    )
    filter_bands(cot_pieces, 0, adjoint, rows, basis, filtered)
    total = None
    for k in range(basis):
        term = lax.dot_general(
            filtered[:, k * channels : (k + 1) * channels],
            mixing[k],
            (((1,), (1,)), ((), ())),
            preferred_element_type=jnp.float32,
        )
        total = term if total is None else total + term
    by_row(total, wide, grad_states)


def chips_apart(x):
    return lax.ppermute(x, LAT, steps(2)), lax.ppermute(x, LAT, steps(-2))


def far_and_near(x):
    far = [p for p in steps(3) if p[0] % 2 == 1] + [p for p in steps(-3) if p[0] % 2 == 0]
    return lax.ppermute(x, LAT, far), from_mate(x)


def from_mate(x):
    return lax.ppermute(x, LAT, [(i, i ^ 1) for i in range(lax.axis_size(LAT))])


def steps(by):
    count = lax.axis_size(LAT)
    return [(i, i + by) for i in range(count) if 0 <= i + by < count]


def scattered(parts):
    return lax.all_to_all(parts, PLANE, 0, 0).astype(jnp.float32).sum(0).astype(jnp.bfloat16)


def gathered(part, axes):
    return lax.all_to_all(jnp.broadcast_to(part[None], (lax.axis_size(axes),) + part.shape), axes, 0, 0)


def shards(states, basis_table, offsets, widths, mixing, cotangent):
    _, rows, cells, channels = states.shape
    basis = mixing.shape[0]
    first_row = lax.axis_index(LAT) * rows
    bf16 = jnp.bfloat16
    tall = jax.ShapeDtypeStruct(((cells + TAPS - 1) * rows, channels), bf16)
    flat = jax.ShapeDtypeStruct((cells * rows, channels), bf16)
    states_wide, cot_wide, cot_own = call(
        prepare_kernel,
        [tall, tall, flat],
        [pltpu.VMEM(tall.shape, jnp.float32)],
        0,
        states[0],
        cotangent[0],
    )
    before, after = chips_apart(states_wide)
    far, mate = far_and_near(states_wide)
    cot_before, cot_after = chips_apart(cot_wide)
    cot_far, cot_mate = far_and_near(cot_wide)

    support, latitudes = basis_table.shape[1], basis_table.shape[0]
    table = basis_table.transpose(2, 3, 1, 0)
    band = jnp.where(lax.axis_index("core") == 0, jnp.array(SLOTS[0]), jnp.array(SLOTS[1]))
    column = first_row + band[:, None, None] * rows + jnp.arange(rows)[None, None, :]
    width = len(SLOTS[0]) * WINDOW * rows
    column = jnp.broadcast_to(column, (len(SLOTS[0]), WINDOW, rows)).reshape(1, width).astype(jnp.int32)
    matrix = jax.ShapeDtypeStruct((basis * GROUP * rows, width), bf16)
    first = first_row.astype(jnp.int32)[None]
    depth = -(-support // 8) * 8
    pairs = -(-basis * rows // 8) * 8
    taken = pltpu.VMEM((TAPS, pairs, latitudes), jnp.float32)
    (forward_wide,) = call(
        lambda *refs: forward_table_kernel(rows, *refs),
        [matrix],
        [pltpu.VMEM((TAPS * depth, latitudes), jnp.float32), taken],
        400_000_000,
        first,
        offsets,
        widths,
        column,
        table,
        scalars=3,
    )
    (adjoint_wide,) = call(
        lambda *refs: adjoint_table_kernel(rows, *refs),
        [matrix],
        [taken],
        400_000_000,
        first,
        offsets[None],
        widths[None],
        column,
        table,
        scalars=1,
    )

    before, after, forward_wide = hold((before, after, forward_wide))
    bands = (far, before, from_mate(before), states_wide, mate, after, from_mate(after))
    plane = lax.axis_size(PLANE)
    (grad,) = call(
        lambda *refs: forward_kernel(rows, *refs),
        [jax.ShapeDtypeStruct((plane * PART, channels), bf16)],
        [pltpu.VMEM((cells * rows, basis * channels), bf16)],
        2_000_000_000,
        *bands,
        forward_wide,
        cot_own,
    )
    part = scattered(grad.reshape(plane, PART, channels))
    part = gathered(part, RING).astype(jnp.float32).sum(0).astype(bf16)
    total = gathered(part, PLANE)
    cot_bands = (cot_far, cot_before, from_mate(cot_before), cot_wide, cot_mate, cot_after, from_mate(cot_after))
    output, grad_states = call(
        lambda *refs: backward_kernel(rows, *refs),
        [jax.ShapeDtypeStruct(states.shape[1:], bf16)] * 2,
        [
            pltpu.VMEM((cells * rows, basis * channels), bf16),
            pltpu.VMEM((cells * rows, channels), jnp.float32),
        ],
        3_000_000_000,
        *bands,
        *cot_bands,
        forward_wide,
        adjoint_wide,
        mixing,
    )
    cell_count = lax.axis_size(DP) * rows * lax.axis_size(LAT) * cells
    grad_scale = 1.0 / math.sqrt(cell_count)
    whole = total.reshape(-1, channels)[: basis * channels].reshape(basis, channels, channels)
    return (output[None], grad_states[None], whole.astype(jnp.float32) * grad_scale)


def solution(mesh):
    fine = Mesh(mesh.devices.reshape(4, 4, 4, 4, 2), DP + LAT)
    banded = P(DP, LAT, None, None)
    in_specs = (banded, P(), P(), P(), P(), banded)
    out_specs = (banded, banded, P())
    return jax.shard_map(shards, mesh=fine, in_specs=in_specs, out_specs=out_specs, check_vma=False)
```
